32 devices in a mesh: pipe: 4 (over y, core), seq: 4 (over z), tp: 2 (over x).
Axes of the slice: x: 2, y: 2, z: 4, core: 2. Of those that a mesh axis runs over, the one named last changes fastest.
Arguments:
- emitted: bfloat16 [4, 512, 8192], P('pipe', 'seq', 'tp'), may hold values from -6 to 6
- cotangent: bfloat16 [4, 512, 8192], P('pipe', 'seq', 'tp'), may hold values from -6 to 6
- b_proj: bfloat16 [4, 512, 512], P('pipe', 'seq', 'tp'), may hold values from -0.26367188 to 0.26367188
- c_proj: bfloat16 [4, 512, 512], P('pipe', 'seq', 'tp'), may hold values from -0.52734375 to 0.52734375
- log_decay: bfloat16 [4, 512, 128], P('pipe', 'seq', 'tp'), may hold values from -1 to 0
- starts: int32 [4, 512], P('pipe', 'seq'), may hold values 0 or 1
- skip: float32 [4, 128], P('pipe', 'tp'), may hold values from 0.5 to 2
Outputs:
- mixed: bfloat16 [4, 512, 8192], P('pipe', 'seq', 'tp')
- input_grad: bfloat16 [4, 512, 8192], P('pipe', 'seq', 'tp')
The draws below stay inside these ranges and needn't reach their ends.
All inputs are finite; a program needn't handle non-finite values. No bound on the sum of `starts` on one device may be relied on, other than what follows from the above.
Results may differ from the reference program's by a relative error of at most 0.001.
Values may be sent and summed in bfloat16 or wider, within the bound.
A program may use at most 64 MiB of HBM per device.

```python
import math
import jax
import jax.numpy as jnp
from jax import lax

TOK_DEV = 128
BLEND_CHANNELS = 128
P_SIZE = 64
N = 128
GROUPS = 4
SPAN = 128
EPISODE_STEPS = 512
HANDOFF_PARTS = 4


def draw_log_decay(key, part):
    stochastic_seeds = jax.random.split(key, 7)
    quick_heads = jax.random.randint(stochastic_seeds[0], (HANDOFF_PARTS, 1, BLEND_CHANNELS), 0, 2) == 0
    quick_rate = jnp.exp(jax.random.uniform(stochastic_seeds[1], (HANDOFF_PARTS, 1, BLEND_CHANNELS), jnp.float32, math.log(1.0 / 50.0), math.log(1.0 / 30.0)))
    slow_rate = jnp.exp(jax.random.uniform(stochastic_seeds[2], (HANDOFF_PARTS, 1, BLEND_CHANNELS), jnp.float32, math.log(0.05), math.log(0.3))) / EPISODE_STEPS
    background_intensity = jnp.where(quick_heads, quick_rate, slow_rate)
    shards = EPISODE_STEPS // TOK_DEV
    partition_scaling = jnp.exp(jax.random.uniform(stochastic_seeds[3], (HANDOFF_PARTS, shards, 1, BLEND_CHANNELS), jnp.float32, 0.0, math.log(3.0)))
    partition_scaling = jnp.broadcast_to(partition_scaling, (HANDOFF_PARTS, shards, TOK_DEV, BLEND_CHANNELS)).reshape(HANDOFF_PARTS, EPISODE_STEPS, BLEND_CHANNELS)
    element_scaling = jax.random.uniform(stochastic_seeds[4], (HANDOFF_PARTS, EPISODE_STEPS, BLEND_CHANNELS), jnp.float32, 0.5, 1.5)
    spike_locations = jax.random.randint(stochastic_seeds[5], (HANDOFF_PARTS, 2, BLEND_CHANNELS), 0, EPISODE_STEPS)
    spike_amplitudes = jnp.exp(jax.random.uniform(stochastic_seeds[6], (HANDOFF_PARTS, 2, BLEND_CHANNELS), jnp.float32, math.log(0.22), math.log(0.69)))
    location_table = jnp.arange(EPISODE_STEPS)[None, :, None]
    spike_occurrences = (location_table == spike_locations[:, 0:1, :]) * spike_amplitudes[:, 0:1, :] + (location_table == spike_locations[:, 1:2, :]) * spike_amplitudes[:, 1:2, :]
    combined = -(background_intensity * partition_scaling * element_scaling) - spike_occurrences
    return jnp.maximum(combined, -0.99).astype(jnp.bfloat16)


def touch_ends(array, own_key, low, largest):
    place = [jax.random.randint(jax.random.fold_in(own_key, axis), (), 0, length) for axis, length in enumerate(array.shape)]
    widest = array.shape.index(max(array.shape))
    neighbour = place[:widest] + [(place[widest] + 1) % array.shape[widest]] + place[widest + 1:]
    return array.at[tuple(place)].set(low).at[tuple(neighbour)].set(largest)


def steps_of(stream_key, dims, cuts, smallest, high):
    def one(dim, parts):
        heights = jax.random.uniform(jax.random.fold_in(jax.random.fold_in(stream_key, 6), dim), (parts,), jnp.float32, smallest / len(cuts), high / len(cuts))
        return jnp.repeat(jnp.exp(heights), dims[dim] // parts).reshape((-1,) + (1,) * (len(dims) - dim - 1))

    loudness = one(*cuts[0])
    for cut in cuts[1:]:
        loudness = loudness * one(*cut)
    return loudness


def bell_draw(key, shape, scale, bound, cuts=(), dtype=jnp.bfloat16):
    values = jax.random.normal(key, shape, jnp.float32) * scale
    if len(cuts) > 0:
        values = steps_of(key, shape, cuts, -0.22, 0.18) * values
    return jnp.clip(values, min=-bound, max=bound).astype(dtype)


def setup_inputs(seed: int = 0) -> dict:
    key_list = jax.random.split(jax.random.key(seed), 8)
    emitted = bell_draw(key_list[0], (HANDOFF_PARTS, EPISODE_STEPS, BLEND_CHANNELS * P_SIZE), 1.0, 6.0, ((0, 4), (1, 4), (2, 2)))
    cotangent = bell_draw(key_list[1], (HANDOFF_PARTS, EPISODE_STEPS, BLEND_CHANNELS * P_SIZE), 1.0, 6.0, ((0, 4), (1, 4), (2, 2)))
    b_proj = bell_draw(key_list[2], (HANDOFF_PARTS, EPISODE_STEPS, GROUPS * N), (0.5 * N ** -0.5), 0.26367188, ((0, 4), (1, 4), (2, 2)))
    c_proj = bell_draw(key_list[3], (HANDOFF_PARTS, EPISODE_STEPS, GROUPS * N), (N ** -0.5), 0.52734375, ((0, 4), (1, 4), (2, 2)))
    log_decay = draw_log_decay(jax.random.fold_in(key_list[7], 71), 0)
    starts = touch_ends((jax.random.randint(key_list[5], (HANDOFF_PARTS, EPISODE_STEPS), 0, 4 * TOK_DEV) < 1).astype(jnp.int32), jax.random.fold_in(key_list[5], 1), 0, 1)
    skip = jnp.clip(jnp.exp(math.log(2.0) - 1.3862944 * jax.random.uniform(key_list[6], (HANDOFF_PARTS, BLEND_CHANNELS), jnp.float32) ** steps_of(key_list[6], (HANDOFF_PARTS, BLEND_CHANNELS), ((0, 4), (1, 2)), -0.2, 0.2)), 0.5, 2.0)
    return {"emitted": emitted, "cotangent": cotangent, "b_proj": b_proj, "c_proj": c_proj, "log_decay": log_decay, "starts": starts, "skip": skip}


HIGH = lax.Precision.HIGHEST


def single_terms(inputs, upstream, b_rows, c_rows, decay_rows, opened):
    running = jnp.cumsum(decay_rows, axis=1)
    running_end = running[:, -1]
    opened_sum = jnp.cumsum(opened, axis=1)
    opened_end = opened_sum[:, -1]
    width = inputs.shape[1]
    causal = jnp.arange(width)[:, None] >= jnp.arange(width)[None, :]
    linked = (opened_sum[:, :, None] == opened_sum[:, None, :]) & causal[None]
    spread = running[:, :, None] - running[:, None, :]
    damping = jnp.where(linked[:, :, :, None, None], jnp.exp(jnp.minimum(spread, 0.0)), 0.0)
    intersection = jnp.einsum("ktgn,ksgn->ktsg", c_rows, b_rows, precision=HIGH)
    mixing = damping * intersection[..., None]
    mixed_part = jnp.einsum("ktsge,ksgep->ktgep", mixing, inputs, precision=HIGH)
    grad_part = jnp.einsum("ktsge,ktgep->ksgep", mixing, upstream, precision=HIGH)
    inflow = jnp.exp(running) * (opened_sum == 0.0)[:, :, None, None]
    outflow = jnp.exp(running_end[:, None] - running) * (opened_sum == opened_end[:, None])[:, :, None, None]
    through = jnp.exp(running_end) * (opened_end == 0.0)[:, None, None]
    end_states = jnp.einsum("ksgn,ksgep->kgenp", b_rows, inputs * outflow[..., None], precision=HIGH)
    start_states = jnp.einsum("ksgn,ksgep->kgenp", c_rows, upstream * inflow[..., None], precision=HIGH)
    return mixed_part, grad_part, inflow, outflow, through, end_states, start_states


def block_terms(inputs, upstream, b_rows, c_rows, decay_rows, opened):
    def one_block(pieces):
        result = single_terms(*[piece[None] for piece in pieces])
        return tuple(item[0] for item in result)
    return lax.map(one_block, (inputs, upstream, b_rows, c_rows, decay_rows, opened))


def pass_forward(through, end_states, first_state):
    def advance(current, element):
        return element[0][:, :, None, None] * current + element[1], current
    final, entering = lax.scan(advance, first_state, (through, end_states))
    return entering, final


def pass_backward(through, start_states, last_state):
    def advance(current, element):
        return element[0][:, :, None, None] * current + element[1], current
    final, leaving = lax.scan(advance, last_state, (through, start_states), reverse=True)
    return leaving, final


def finish(terms, inputs, upstream, b_rows, c_rows, skip_gain, first_state, last_state):
    mixed_part, grad_part, inflow, outflow, through, end_states, start_states = terms
    entering, _ = pass_forward(through, end_states, first_state)
    leaving, _ = pass_backward(through, start_states, last_state)
    gain_wide = skip_gain[None, None, :, :, None]
    mixed = mixed_part + jnp.einsum("ktgn,kgenp->ktgep", c_rows, entering, precision=HIGH) * inflow[..., None] + gain_wide * inputs
    grads = grad_part + jnp.einsum("ktgn,kgenp->ktgep", b_rows, leaving, precision=HIGH) * outflow[..., None] + gain_wide * upstream
    return mixed, grads


def section(pieces):
    inputs, upstream, b_proj, c_proj, log_decay, starts, skip = pieces
    block_count = EPISODE_STEPS // SPAN
    per_group = BLEND_CHANNELS // GROUPS
    blocked = (block_count, SPAN, GROUPS, per_group, P_SIZE)
    values = inputs.astype(jnp.float32).reshape(blocked)
    grads_in = upstream.astype(jnp.float32).reshape(blocked)
    b_rows = b_proj.astype(jnp.float32).reshape(block_count, SPAN, GROUPS, N)
    c_rows = c_proj.astype(jnp.float32).reshape(block_count, SPAN, GROUPS, N)
    decay_rows = log_decay.astype(jnp.float32).reshape(block_count, SPAN, GROUPS, per_group)
    opened = starts.astype(jnp.float32).reshape(block_count, SPAN)
    skip_gain = skip.reshape(GROUPS, per_group)
    terms = block_terms(values, grads_in, b_rows, c_rows, decay_rows, opened)
    empty_state = jnp.zeros((GROUPS, per_group, N, P_SIZE), jnp.float32)
    mixed, grads = finish(terms, values, grads_in, b_rows, c_rows, skip_gain, empty_state, empty_state)
    return (mixed.reshape(EPISODE_STEPS, BLEND_CHANNELS * P_SIZE).astype(jnp.bfloat16), grads.reshape(EPISODE_STEPS, BLEND_CHANNELS * P_SIZE).astype(jnp.bfloat16))


def reference(emitted, cotangent, b_proj, c_proj, log_decay, starts, skip):
    inputs = jnp.concatenate([emitted[:1], emitted[:-1]], axis=0)
    mixed, input_grad = lax.map(section, (inputs, cotangent, b_proj, c_proj, log_decay, starts, skip))
    return mixed, input_grad
```

```python
import functools

import jax
import jax.numpy as jnp
from jax import lax
from jax.experimental import pallas as pl
from jax.experimental.pallas import tpu as pltpu
from jax.sharding import PartitionSpec as P

BLEND_CHANNELS = 128
P_SIZE = 64
N = 128
GROUPS = 4
COLS = 512
MESH = pl.DeviceIdType.MESH
F32 = jnp.float32
BF16 = jnp.bfloat16


def split(value):
    high = value.astype(BF16)
    return high, (value - high.astype(F32)).astype(BF16)


def dot(a, b):
    return jnp.dot(a, b, preferred_element_type=F32)


def kernel(
    pipe_count, seq_count, cols,
    e_ref, g_ref, b_ref, c_ref, d_ref, st_ref, sk_ref,
    mixed_ref, grad_ref,
    x_buf, up_out, up_in, down_out, down_in,
    small, centre, lhs_up, lhs_down, low_up, low_down, enter_up, enter_down,
    part_up, part_down, own_up, own_down, gone_row,
    x_send, x_recv, up_send, up_recv, down_send, down_recv,
):
    length = e_ref.shape[1]
    chunks = e_ref.shape[2] // cols
    heads = sk_ref.shape[1]
    group_count = b_ref.shape[2] // N
    chunk_heads = cols // P_SIZE
    chunks_per_group = chunks // group_count
    middle = length // 2 - 1
    pipe = lax.axis_index("pipe")
    seq = lax.axis_index("seq")
    has_prev_pipe, has_next_pipe = pipe > 0, pipe < pipe_count - 1
    has_prev, has_next = seq > 0, seq < seq_count - 1

    barrier = pltpu.get_barrier_semaphore()

    def greet(present, where):
        @pl.when(present)
        def _():
            pl.semaphore_signal(barrier, inc=1, device_id=where, device_id_type=MESH)

    greet(has_prev_pipe, {"pipe": pipe - 1})
    greet(has_next_pipe, {"pipe": pipe + 1})
    greet(has_prev, {"seq": seq - 1})
    greet(has_next, {"seq": seq + 1})
    count = (
        has_prev_pipe.astype(jnp.int32) + has_next_pipe.astype(jnp.int32)
        + has_prev.astype(jnp.int32) + has_next.astype(jnp.int32)
    )
    pl.semaphore_wait(barrier, count)

    def x_copy(j):
        return pltpu.make_async_remote_copy(
            src_ref=e_ref.at[0, :, pl.ds(pl.multiple_of(j * cols, cols), cols)],
            dst_ref=x_buf.at[j],
            send_sem=x_send.at[j], recv_sem=x_recv.at[j],
            device_id={"pipe": pipe + 1}, device_id_type=MESH,
        )

    def up_copy(j):
        return pltpu.make_async_remote_copy(
            src_ref=up_out.at[j], dst_ref=up_in.at[j],
            send_sem=up_send.at[j], recv_sem=up_recv.at[j],
            device_id={"seq": seq + 1}, device_id_type=MESH,
        )

    def down_copy(j):
        return pltpu.make_async_remote_copy(
            src_ref=down_out.at[j], dst_ref=down_in.at[j],
            send_sem=down_send.at[j], recv_sem=down_recv.at[j],
            device_id={"seq": seq - 1}, device_id_type=MESH,
        )

    @pl.when(has_next_pipe)
    def _():
        @pl.loop(0, chunks)
        def _(j):
            x_copy(j).start()

    row = lax.broadcasted_iota(jnp.int32, (length, length), 0)
    col = lax.broadcasted_iota(jnp.int32, (length, length), 1)
    starts_row = st_ref[...].astype(F32)
    starts_col = jnp.sum(jnp.where(row == col, starts_row, 0.0), axis=1, keepdims=True)
    opened_col = jnp.sum(jnp.where(col <= row, starts_row, 0.0), axis=1, keepdims=True)
    opened_row = jnp.sum(jnp.where(row <= col, starts_col, 0.0), axis=0, keepdims=True)
    opened_end = jnp.sum(starts_row, axis=1, keepdims=True)
    same = opened_col == opened_row
    link_up = jnp.logical_and(same, col <= row)
    link_down = jnp.logical_and(same, row <= col)
    in_mask = jnp.where(opened_col == 0.0, 1.0, 0.0)
    out_mask = jnp.where(opened_col == opened_end, 1.0, 0.0)
    gone_row[...] = jnp.broadcast_to(jnp.where(opened_end == 0.0, 1.0, 0.0), gone_row.shape)
    centre[...] = (
        jnp.where(col <= row, 1.0, 0.0) - jnp.where(col <= middle, 1.0, 0.0)
    ).astype(BF16)
    small[0:length, :] = d_ref[0]
    gain = sk_ref[...]
    gain_high = gain.astype(BF16).astype(F32)
    gain_mid = (gain - gain_high).astype(BF16).astype(F32)
    gain_low = gain - gain_high - gain_mid
    gain_row = lax.broadcasted_iota(jnp.int32, (16, heads), 0)
    small[length:, :] = jnp.where(
        gain_row == 0, gain_high,
        jnp.where(gain_row == 1, gain_mid, jnp.where(gain_row == 2, gain_low, 0.0)),
    ).astype(BF16)
    for q in range(group_count):
        b = b_ref[0, :, q * N:(q + 1) * N]
        c = c_ref[0, :, q * N:(q + 1) * N]
        contract = (((1,), (1,)), ((), ()))
        cross_up = lax.dot_general(c, b, contract, preferred_element_type=F32)
        cross_down = lax.dot_general(b, c, contract, preferred_element_type=F32)
        high, low = split(jnp.where(link_up, cross_up, 0.0))
        lhs_up[q, 0:length, 0:length] = high
        lhs_up[q, 0:length, length:] = high
        low_up[q] = low
        high, low = split(jnp.where(link_down, cross_down, 0.0))
        lhs_down[q, 0:length, 0:length] = high
        lhs_down[q, 0:length, length:] = high
        low_down[q] = low
        b_kept = b.astype(F32) * out_mask
        c_kept = c.astype(F32) * in_mask
        b_turned = b_kept.T.astype(BF16)
        c_turned = c_kept.T.astype(BF16)
        lhs_up[q, length:, 0:length] = b_turned
        lhs_up[q, length:, length:] = b_turned
        lhs_down[q, length:, 0:length] = c_turned
        lhs_down[q, length:, length:] = c_turned
        enter_up[q, :, 0:N] = c_kept.astype(BF16)
        enter_up[q, :, N:] = c_kept.astype(BF16)
        enter_down[q, :, 0:N] = b_kept.astype(BF16)
        enter_down[q, :, N:] = b_kept.astype(BF16)

    def factors(j):
        own = lax.broadcasted_iota(jnp.int32, (heads, cols), 0)
        lane = lax.broadcasted_iota(jnp.int32, (heads, cols), 1)
        first = own * P_SIZE - j * cols
        pick = jnp.logical_and(lane >= first, lane < first + P_SIZE)
        wide = dot(small[...], jnp.where(pick, 1.0, 0.0).astype(BF16))
        decay = wide[0:length]
        gain_wide = jnp.sum(wide[length:], axis=0, keepdims=True)
        shift = dot(centre[...], decay.astype(BF16))
        half = decay[0:1] - shift[0:1]
        return shift, half, gain_wide

    steps = chunks + seq_count - 1

    @pl.loop(0, steps)
    def _(step):
        ju = step - seq
        jd = step - (seq_count - 1 - seq)
        up_on = jnp.logical_and(ju >= 0, ju < chunks)
        down_on = jnp.logical_and(jd >= 0, jd < chunks)

        @pl.when(down_on)
        def _():
            q = jd // chunks_per_group
            shift, half, gain_wide = factors(jd)
            g = g_ref[0, :, pl.ds(pl.multiple_of(jd * cols, cols), cols)].astype(F32)
            high, low = split(g * jnp.exp(shift))
            both = dot(lhs_down[q], jnp.concatenate([high, low], axis=0))
            back = jnp.exp(-shift)
            part_down[0] = (both[0:length] + dot(low_down[q], high)) * back + gain_wide * g
            part_down[1] = back * jnp.exp(shift[length - 1:])
            own_down[0:N] = both[length:] * jnp.exp(half)
            own_down[N:N + 8] = jnp.broadcast_to(
                jnp.exp(half + shift[length - 1:]) * gone_row[0:1, 0:1], (8, cols)
            )

            @pl.when(seq == seq_count - 1)
            def _():
                down_in[jd] = jnp.zeros(down_in.shape[1:], BF16)

        @pl.when(up_on)
        def _():
            q = ju // chunks_per_group

            @pl.when(pipe == 0)
            def _():
                x_buf[ju] = e_ref[0, :, pl.ds(pl.multiple_of(ju * cols, cols), cols)]

            @pl.when(has_prev_pipe)
            def _():
                x_copy(ju).wait_recv()

            shift, half, gain_wide = factors(ju)
            x = x_buf[ju].astype(F32)
            high, low = split(x * jnp.exp(-shift))
            both = dot(lhs_up[q], jnp.concatenate([high, low], axis=0))
            forth = jnp.exp(shift)
            part_up[0] = (both[0:length] + dot(low_up[q], high)) * forth + gain_wide * x
            part_up[1] = forth * jnp.exp(half)
            own_up[0:N] = both[length:] * jnp.exp(shift[length - 1:])
            own_up[N:N + 8] = jnp.broadcast_to(
                jnp.exp(half + shift[length - 1:]) * gone_row[0:1, 0:1], (8, cols)
            )

            @pl.when(seq == 0)
            def _():
                up_in[ju] = jnp.zeros(up_in.shape[1:], BF16)

        @pl.when(jnp.logical_and(down_on, has_next))
        def _():
            down_copy(jd).wait_recv()

        @pl.when(jnp.logical_and(down_on, has_prev))
        def _():
            got = down_in[jd, 0:N].astype(F32) + down_in[jd, N:].astype(F32)
            high, low = split(got * own_down[N:N + 1] + own_down[0:N])
            down_out[jd, 0:N] = high
            down_out[jd, N:] = low
            down_copy(jd).start()

        @pl.when(jnp.logical_and(up_on, has_prev))
        def _():
            up_copy(ju).wait_recv()

        @pl.when(jnp.logical_and(up_on, has_next))
        def _():
            got = up_in[ju, 0:N].astype(F32) + up_in[ju, N:].astype(F32)
            high, low = split(got * own_up[N:N + 1] + own_up[0:N])
            up_out[ju, 0:N] = high
            up_out[ju, N:] = low
            up_copy(ju).start()

        @pl.when(down_on)
        def _():
            q = jd // chunks_per_group
            total = part_down[0] + dot(enter_down[q], down_in[jd]) * part_down[1]
            grad_ref[0, :, pl.ds(pl.multiple_of(jd * cols, cols), cols)] = total.astype(BF16)

        @pl.when(up_on)
        def _():
            q = ju // chunks_per_group
            total = part_up[0] + dot(enter_up[q], up_in[ju]) * part_up[1]
            mixed_ref[0, :, pl.ds(pl.multiple_of(ju * cols, cols), cols)] = total.astype(BF16)

    @pl.loop(0, chunks)
    def _(j):
        @pl.when(has_next_pipe)
        def _():
            x_copy(j).wait_send()

        @pl.when(has_next)
        def _():
            up_copy(j).wait_send()

        @pl.when(has_prev)
        def _():
            down_copy(j).wait_send()


def body(pipe_count, seq_count, emitted, cotangent, b_proj, c_proj, log_decay, starts, skip):
    _, length, width = emitted.shape
    heads = skip.shape[1]
    group_count = b_proj.shape[2] // N
    cols = COLS
    chunks = width // cols
    whole = pl.BlockSpec(memory_space=pltpu.VMEM)
    dma = pltpu.SemaphoreType.DMA
    return pl.pallas_call(
        functools.partial(kernel, pipe_count, seq_count, cols),
        out_shape=(
            jax.ShapeDtypeStruct(emitted.shape, BF16),
            jax.ShapeDtypeStruct(emitted.shape, BF16),
        ),
        in_specs=[whole] * 7,
        out_specs=(whole, whole),
        scratch_shapes=[
            pltpu.VMEM((chunks, length, cols), BF16),
            pltpu.VMEM((chunks, 2 * N, cols), BF16),
            pltpu.VMEM((chunks, 2 * N, cols), BF16),
            pltpu.VMEM((chunks, 2 * N, cols), BF16),
            pltpu.VMEM((chunks, 2 * N, cols), BF16),
            pltpu.VMEM((length + 16, heads), BF16),
            pltpu.VMEM((length, length), BF16),
            pltpu.VMEM((group_count, length + N, 2 * length), BF16),
            pltpu.VMEM((group_count, length + N, 2 * length), BF16),
            pltpu.VMEM((group_count, length, length), BF16),
            pltpu.VMEM((group_count, length, length), BF16),
            pltpu.VMEM((group_count, length, 2 * N), BF16),
            pltpu.VMEM((group_count, length, 2 * N), BF16),
            pltpu.VMEM((2, length, cols), F32),
            pltpu.VMEM((2, length, cols), F32),
            pltpu.VMEM((N + 8, cols), F32),
            pltpu.VMEM((N + 8, cols), F32),
            pltpu.VMEM((8, 128), F32),
            dma((chunks,)), dma((chunks,)), dma((chunks,)),
            dma((chunks,)), dma((chunks,)), dma((chunks,)),
        ],
        compiler_params=pltpu.CompilerParams(
            collective_id=0, has_side_effects=True, vmem_limit_bytes=40 * 1024 * 1024
        ),
    )(emitted, cotangent, b_proj, c_proj, log_decay, starts, skip)


def solution(mesh):
    wide = P("pipe", "seq", "tp")
    return jax.shard_map(
        functools.partial(body, mesh.shape["pipe"], mesh.shape["seq"]),
        mesh=mesh,
        in_specs=(wide, wide, wide, wide, wide, P("pipe", "seq"), P("pipe", "tp")),
        out_specs=(wide, wide),
        check_vma=False,
    )
```

```python
import functools

import jax
import jax.numpy as jnp
from jax import lax
from jax.experimental import pallas as pl
from jax.experimental.pallas import tpu as pltpu
from jax.sharding import PartitionSpec as P

BLEND_CHANNELS = 128
P_SIZE = 64
CODE_MAX = 32000.0
N = 128
GROUPS = 4
COLS = 512
LAG = 2
MESH = pl.DeviceIdType.MESH
F32 = jnp.float32
BF16 = jnp.bfloat16


def split(value):
    high = value.astype(BF16)
    return high, (value - high.astype(F32)).astype(BF16)


def dot(a, b):
    return jnp.dot(a, b, preferred_element_type=F32)


def kernel(
    pipe_count, seq_count, cols,
    e_ref, g_ref, b_ref, c_ref, d_ref, st_ref, sk_ref,
    mixed_ref, grad_ref,
    x_buf, up_out, up_in, down_out, down_in,
    up_scale_out, up_scale_in, down_scale_out, down_scale_in, got_up, got_down,
    small, centre, lhs_up, lhs_down, low_up, low_down, enter_up, enter_down,
    part_up, part_down, own_up, own_down, gone_row,
    x_send, x_recv, up_send, up_recv, down_send, down_recv,
    up_scale_send, up_scale_recv, down_scale_send, down_scale_recv,
):
    length = e_ref.shape[1]
    chunks = e_ref.shape[2] // cols
    heads = sk_ref.shape[1]
    group_count = b_ref.shape[2] // N
    chunk_heads = cols // P_SIZE
    chunks_per_group = chunks // group_count
    middle = length // 2 - 1
    pipe = lax.axis_index("pipe")
    seq = lax.axis_index("seq")
    has_prev_pipe, has_next_pipe = pipe > 0, pipe < pipe_count - 1
    has_prev, has_next = seq > 0, seq < seq_count - 1

    barrier = pltpu.get_barrier_semaphore()

    def greet(present, where):
        @pl.when(present)
        def _():
            pl.semaphore_signal(barrier, inc=1, device_id=where, device_id_type=MESH)

    greet(has_prev_pipe, {"pipe": pipe - 1})
    greet(has_next_pipe, {"pipe": pipe + 1})
    greet(has_prev, {"seq": seq - 1})
    greet(has_next, {"seq": seq + 1})
    count = (
        has_prev_pipe.astype(jnp.int32) + has_next_pipe.astype(jnp.int32)
        + has_prev.astype(jnp.int32) + has_next.astype(jnp.int32)
    )
    pl.semaphore_wait(barrier, count)

    def x_copy(j):
        return pltpu.make_async_remote_copy(
            src_ref=e_ref.at[0, :, pl.ds(pl.multiple_of(j * cols, cols), cols)],
            dst_ref=x_buf.at[j],
            send_sem=x_send.at[j], recv_sem=x_recv.at[j],
            device_id={"pipe": pipe + 1}, device_id_type=MESH,
        )

    def pair(pieces, where):
        return [
            pltpu.make_async_remote_copy(
                src_ref=source, dst_ref=target, send_sem=sent, recv_sem=arrived,
                device_id=where, device_id_type=MESH,
            )
            for source, target, sent, arrived in pieces
        ]

    def up_copies(j):
        return pair([
            (up_scale_out.at[j], up_scale_in.at[j], up_scale_send.at[j], up_scale_recv.at[j]),
            (up_out.at[j], up_in.at[j], up_send.at[j], up_recv.at[j]),
        ], {"seq": seq + 1})

    def down_copies(j):
        return pair([
            (down_scale_out.at[j], down_scale_in.at[j], down_scale_send.at[j],
             down_scale_recv.at[j]),
            (down_out.at[j], down_in.at[j], down_send.at[j], down_recv.at[j]),
        ], {"seq": seq - 1})

    @pl.when(has_next_pipe)
    def _():
        @pl.loop(0, chunks)
        def _(j):
            x_copy(j).start()

    row = lax.broadcasted_iota(jnp.int32, (length, length), 0)
    col = lax.broadcasted_iota(jnp.int32, (length, length), 1)
    starts_row = st_ref[...].astype(F32)
    starts_col = jnp.sum(jnp.where(row == col, starts_row, 0.0), axis=1, keepdims=True)
    opened_col = jnp.sum(jnp.where(col <= row, starts_row, 0.0), axis=1, keepdims=True)
    opened_row = jnp.sum(jnp.where(row <= col, starts_col, 0.0), axis=0, keepdims=True)
    opened_end = jnp.sum(starts_row, axis=1, keepdims=True)
    same = opened_col == opened_row
    link_up = jnp.logical_and(same, col <= row)
    link_down = jnp.logical_and(same, row <= col)
    in_mask = jnp.where(opened_col == 0.0, 1.0, 0.0)
    out_mask = jnp.where(opened_col == opened_end, 1.0, 0.0)
    gone_row[...] = jnp.broadcast_to(jnp.where(opened_end == 0.0, 1.0, 0.0), gone_row.shape)
    centre[...] = (
        jnp.where(col <= row, 1.0, 0.0) - jnp.where(col <= middle, 1.0, 0.0)
    ).astype(BF16)
    small[0:length, :] = d_ref[0]
    gain = sk_ref[...]
    gain_high = gain.astype(BF16).astype(F32)
    gain_mid = (gain - gain_high).astype(BF16).astype(F32)
    gain_low = gain - gain_high - gain_mid
    gain_row = lax.broadcasted_iota(jnp.int32, (16, heads), 0)
    small[length:, :] = jnp.where(
        gain_row == 0, gain_high,
        jnp.where(gain_row == 1, gain_mid, jnp.where(gain_row == 2, gain_low, 0.0)),
    ).astype(BF16)
    for q in range(group_count):
        b = b_ref[0, :, q * N:(q + 1) * N]
        c = c_ref[0, :, q * N:(q + 1) * N]
        contract = (((1,), (1,)), ((), ()))
        cross_up = lax.dot_general(c, b, contract, preferred_element_type=F32)
        cross_down = lax.dot_general(b, c, contract, preferred_element_type=F32)
        high, low = split(jnp.where(link_up, cross_up, 0.0))
        lhs_up[q, 0:length, 0:length] = high
        lhs_up[q, 0:length, length:] = high
        low_up[q] = low
        high, low = split(jnp.where(link_down, cross_down, 0.0))
        lhs_down[q, 0:length, 0:length] = high
        lhs_down[q, 0:length, length:] = high
        low_down[q] = low
        b_kept = b.astype(F32) * out_mask
        c_kept = c.astype(F32) * in_mask
        b_turned = b_kept.T.astype(BF16)
        c_turned = c_kept.T.astype(BF16)
        lhs_up[q, length:, 0:length] = b_turned
        lhs_up[q, length:, length:] = b_turned
        lhs_down[q, length:, 0:length] = c_turned
        lhs_down[q, length:, length:] = c_turned
        enter_up[q, :, 0:N] = c_kept.astype(BF16)
        enter_up[q, :, N:] = c_kept.astype(BF16)
        enter_down[q, :, 0:N] = b_kept.astype(BF16)
        enter_down[q, :, N:] = b_kept.astype(BF16)

    def factors(j):
        own = lax.broadcasted_iota(jnp.int32, (heads, cols), 0)
        lane = lax.broadcasted_iota(jnp.int32, (heads, cols), 1)
        first = own * P_SIZE - j * cols
        pick = jnp.logical_and(lane >= first, lane < first + P_SIZE)
        wide = dot(small[...], jnp.where(pick, 1.0, 0.0).astype(BF16))
        decay = wide[0:length]
        gain_wide = jnp.sum(wide[length:], axis=0, keepdims=True)
        shift = dot(centre[...], decay.astype(BF16))
        half = decay[0:1] - shift[0:1]
        return shift, half, gain_wide

    steps = chunks + LAG * (seq_count - 1)

    @pl.loop(0, steps)
    def _(step):
        ju = step - LAG * seq
        jd = step - LAG * (seq_count - 1 - seq)
        up_on = jnp.logical_and(ju >= 0, ju < chunks)
        down_on = jnp.logical_and(jd >= 0, jd < chunks)

        @pl.when(step < chunks)
        def _():
            j = step
            q = j // chunks_per_group
            shift, half, gain_wide = factors(j)
            forth, back = jnp.exp(shift), jnp.exp(-shift)
            forth_end, forth_in = jnp.exp(shift[length - 1:]), jnp.exp(half)
            gone = jnp.exp(half + shift[length - 1:]) * gone_row[0:1, 0:1]
            g = g_ref[0, :, pl.ds(pl.multiple_of(j * cols, cols), cols)].astype(F32)
            high, low = split(g * forth)
            both = dot(lhs_down[q], jnp.concatenate([high, low], axis=0))
            part_down[j, 0] = (both[0:length] + dot(low_down[q], high)) * back + gain_wide * g
            part_down[j, 1] = back * forth_end
            own_down[j, 0:N] = both[length:] * forth_in
            own_down[j, N:N + 8] = jnp.broadcast_to(gone, (8, cols))

            @pl.when(pipe == 0)
            def _():
                x_buf[j] = e_ref[0, :, pl.ds(pl.multiple_of(j * cols, cols), cols)]

            @pl.when(has_prev_pipe)
            def _():
                x_copy(j).wait_recv()

            x = x_buf[j].astype(F32)
            high, low = split(x * back)
            both = dot(lhs_up[q], jnp.concatenate([high, low], axis=0))
            part_up[j, 0] = (both[0:length] + dot(low_up[q], high)) * forth + gain_wide * x
            part_up[j, 1] = forth * forth_in
            own_up[j, 0:N] = both[length:] * forth_end
            own_up[j, N:N + 8] = jnp.broadcast_to(gone, (8, cols))

        def relay(on, j, source, target, copies, code_in, scale_in, code_out, scale_out, got, own):
            @pl.when(on)
            def _():
                @pl.when(jnp.logical_not(source))
                def _():
                    got[...] = jnp.zeros(got.shape, F32)

                @pl.when(source)
                def _():
                    for copy in copies(j):
                        copy.wait_recv()
                    scale = jnp.sum(
                        jnp.where(row == col, scale_in[j, 0:1], 0.0), axis=1, keepdims=True
                    )
                    got[...] = code_in[j].astype(jnp.int32).astype(F32) * scale

                @pl.when(target)
                def _():
                    state = got[...] * own[j, N:N + 1] + own[j, 0:N]
                    largest = jnp.maximum(
                        jnp.max(jnp.abs(state), axis=1, keepdims=True), 1e-30
                    )
                    code = jnp.round(state * (CODE_MAX / largest))
                    code_out[j] = code.astype(jnp.int32).astype(jnp.int16)
                    scale = jnp.sum(
                        jnp.where(row == col, largest * (1.0 / CODE_MAX), 0.0),
                        axis=0, keepdims=True,
                    )
                    scale_out[j] = jnp.broadcast_to(scale, scale_out.shape[1:])
                    for copy in copies(j):
                        copy.start()

        relay(down_on, jd, has_next, has_prev, down_copies, down_in, down_scale_in,
              down_out, down_scale_out, got_down, own_down)
        relay(up_on, ju, has_prev, has_next, up_copies, up_in, up_scale_in,
              up_out, up_scale_out, got_up, own_up)

        @pl.when(down_on)
        def _():
            q = jd // chunks_per_group
            both = jnp.concatenate(split(got_down[...]), axis=0)
            total = part_down[jd, 0] + dot(enter_down[q], both) * part_down[jd, 1]
            grad_ref[0, :, pl.ds(pl.multiple_of(jd * cols, cols), cols)] = total.astype(BF16)

        @pl.when(up_on)
        def _():
            q = ju // chunks_per_group
            both = jnp.concatenate(split(got_up[...]), axis=0)
            total = part_up[ju, 0] + dot(enter_up[q], both) * part_up[ju, 1]
            mixed_ref[0, :, pl.ds(pl.multiple_of(ju * cols, cols), cols)] = total.astype(BF16)

    @pl.loop(0, chunks)
    def _(j):
        @pl.when(has_next_pipe)
        def _():
            x_copy(j).wait_send()

        @pl.when(has_next)
        def _():
            for copy in up_copies(j):
                copy.wait_send()

        @pl.when(has_prev)
        def _():
            for copy in down_copies(j):
                copy.wait_send()


def body(pipe_count, seq_count, emitted, cotangent, b_proj, c_proj, log_decay, starts, skip):
    _, length, width = emitted.shape
    heads = skip.shape[1]
    group_count = b_proj.shape[2] // N
    cols = COLS
    chunks = width // cols
    whole = pl.BlockSpec(memory_space=pltpu.VMEM)
    dma = pltpu.SemaphoreType.DMA
    return pl.pallas_call(
        functools.partial(kernel, pipe_count, seq_count, cols),
        out_shape=(
            jax.ShapeDtypeStruct(emitted.shape, BF16),
            jax.ShapeDtypeStruct(emitted.shape, BF16),
        ),
        in_specs=[whole] * 7,
        out_specs=(whole, whole),
        scratch_shapes=[
            pltpu.VMEM((chunks, length, cols), BF16),
            pltpu.VMEM((chunks, N, cols), jnp.int16),
            pltpu.VMEM((chunks, N, cols), jnp.int16),
            pltpu.VMEM((chunks, N, cols), jnp.int16),
            pltpu.VMEM((chunks, N, cols), jnp.int16),
            pltpu.VMEM((chunks, 8, N), F32),
            pltpu.VMEM((chunks, 8, N), F32),
            pltpu.VMEM((chunks, 8, N), F32),
            pltpu.VMEM((chunks, 8, N), F32),
            pltpu.VMEM((N, cols), F32),
            pltpu.VMEM((N, cols), F32),
            pltpu.VMEM((length + 16, heads), BF16),
            pltpu.VMEM((length, length), BF16),
            pltpu.VMEM((group_count, length + N, 2 * length), BF16),
            pltpu.VMEM((group_count, length + N, 2 * length), BF16),
            pltpu.VMEM((group_count, length, length), BF16),
            pltpu.VMEM((group_count, length, length), BF16),
            pltpu.VMEM((group_count, length, 2 * N), BF16),
            pltpu.VMEM((group_count, length, 2 * N), BF16),
            pltpu.VMEM((chunks, 2, length, cols), F32),
            pltpu.VMEM((chunks, 2, length, cols), F32),
            pltpu.VMEM((chunks, N + 8, cols), F32),
            pltpu.VMEM((chunks, N + 8, cols), F32),
            pltpu.VMEM((8, 128), F32),
            dma((chunks,)), dma((chunks,)), dma((chunks,)),
            dma((chunks,)), dma((chunks,)), dma((chunks,)),
            dma((chunks,)), dma((chunks,)), dma((chunks,)), dma((chunks,)),
        ],
        compiler_params=pltpu.CompilerParams(
            collective_id=0, has_side_effects=True, vmem_limit_bytes=40 * 1024 * 1024
        ),
    )(emitted, cotangent, b_proj, c_proj, log_decay, starts, skip)


def solution(mesh):
    wide = P("pipe", "seq", "tp")
    return jax.shard_map(
        functools.partial(body, mesh.shape["pipe"], mesh.shape["seq"]),
        mesh=mesh,
        in_specs=(wide, wide, wide, wide, wide, P("pipe", "seq"), P("pipe", "tp")),
        out_specs=(wide, wide),
        check_vma=False,
    )
```

```python
import functools

import jax
import jax.numpy as jnp
from jax import lax
from jax.experimental import pallas as pl
from jax.experimental.pallas import tpu as pltpu
from jax.sharding import PartitionSpec as P

BLEND_CHANNELS = 128
P_SIZE = 64
CODE_MAX = 32000.0
N = 128
GROUPS = 4
COLS = 512
LAG = 2
UP_DELAY = 0
MESH = pl.DeviceIdType.MESH
F32 = jnp.float32
BF16 = jnp.bfloat16


def split(value):
    high = value.astype(BF16)
    return high, (value - high.astype(F32)).astype(BF16)


def dot(a, b):
    return jnp.dot(a, b, preferred_element_type=F32)


def kernel(
    pipe_count, seq_count, cols,
    e_ref, g_ref, b_ref, c_ref, d_ref, st_ref, sk_ref,
    mixed_ref, grad_ref,
    x_buf, up_out, up_in, down_out, down_in,
    up_scale_out, up_scale_in, down_scale_out, down_scale_in, got_up, got_down,
    small, centre, lhs_up, lhs_down, low_up, low_down, enter_up, enter_down,
    part_up, part_down, own_up, own_down, gone_row,
    x_send, x_recv, up_send, up_recv, down_send, down_recv,
    up_scale_send, up_scale_recv, down_scale_send, down_scale_recv,
):
    length = e_ref.shape[1]
    chunks = e_ref.shape[2] // cols
    heads = sk_ref.shape[1]
    group_count = b_ref.shape[2] // N
    chunk_heads = cols // P_SIZE
    chunks_per_group = chunks // group_count
    middle = length // 2 - 1
    pipe = lax.axis_index("pipe")
    seq = lax.axis_index("seq")
    has_prev_pipe, has_next_pipe = pipe > 0, pipe < pipe_count - 1
    has_prev, has_next = seq > 0, seq < seq_count - 1

    barrier = pltpu.get_barrier_semaphore()

    def greet(present, where):
        @pl.when(present)
        def _():
            pl.semaphore_signal(barrier, inc=1, device_id=where, device_id_type=MESH)

    greet(has_prev_pipe, {"pipe": pipe - 1})
    greet(has_next_pipe, {"pipe": pipe + 1})
    greet(has_prev, {"seq": seq - 1})
    greet(has_next, {"seq": seq + 1})
    count = (
        has_prev_pipe.astype(jnp.int32) + has_next_pipe.astype(jnp.int32)
        + has_prev.astype(jnp.int32) + has_next.astype(jnp.int32)
    )
    pl.semaphore_wait(barrier, count)

    def x_copy(j):
        return pltpu.make_async_remote_copy(
            src_ref=e_ref.at[0, :, pl.ds(pl.multiple_of(j * cols, cols), cols)],
            dst_ref=x_buf.at[j],
            send_sem=x_send.at[j], recv_sem=x_recv.at[j],
            device_id={"pipe": pipe + 1}, device_id_type=MESH,
        )

    def pair(pieces, where):
        return [
            pltpu.make_async_remote_copy(
                src_ref=source, dst_ref=target, send_sem=sent, recv_sem=arrived,
                device_id=where, device_id_type=MESH,
            )
            for source, target, sent, arrived in pieces
        ]

    def up_copies(j):
        return pair([
            (up_scale_out.at[j], up_scale_in.at[j], up_scale_send.at[j], up_scale_recv.at[j]),
            (up_out.at[j], up_in.at[j], up_send.at[j], up_recv.at[j]),
        ], {"seq": seq + 1})

    def down_copies(j):
        return pair([
            (down_scale_out.at[j], down_scale_in.at[j], down_scale_send.at[j],
             down_scale_recv.at[j]),
            (down_out.at[j], down_in.at[j], down_send.at[j], down_recv.at[j]),
        ], {"seq": seq - 1})

    @pl.when(has_next_pipe)
    def _():
        @pl.loop(0, chunks)
        def _(j):
            x_copy(j).start()

    row = lax.broadcasted_iota(jnp.int32, (length, length), 0)
    col = lax.broadcasted_iota(jnp.int32, (length, length), 1)
    starts_row = st_ref[...].astype(F32)
    starts_col = jnp.sum(jnp.where(row == col, starts_row, 0.0), axis=1, keepdims=True)
    opened_col = jnp.sum(jnp.where(col <= row, starts_row, 0.0), axis=1, keepdims=True)
    opened_row = jnp.sum(jnp.where(row <= col, starts_col, 0.0), axis=0, keepdims=True)
    opened_end = jnp.sum(starts_row, axis=1, keepdims=True)
    same = opened_col == opened_row
    link_up = jnp.logical_and(same, col <= row)
    link_down = jnp.logical_and(same, row <= col)
    in_mask = jnp.where(opened_col == 0.0, 1.0, 0.0)
    out_mask = jnp.where(opened_col == opened_end, 1.0, 0.0)
    gone_row[...] = jnp.broadcast_to(jnp.where(opened_end == 0.0, 1.0, 0.0), gone_row.shape)
    centre[...] = (
        jnp.where(col <= row, 1.0, 0.0) - jnp.where(col <= middle, 1.0, 0.0)
    ).astype(BF16)
    small[0:length, :] = d_ref[0]
    gain = sk_ref[...]
    gain_high = gain.astype(BF16).astype(F32)
    gain_mid = (gain - gain_high).astype(BF16).astype(F32)
    gain_low = gain - gain_high - gain_mid
    gain_row = lax.broadcasted_iota(jnp.int32, (16, heads), 0)
    small[length:, :] = jnp.where(
        gain_row == 0, gain_high,
        jnp.where(gain_row == 1, gain_mid, jnp.where(gain_row == 2, gain_low, 0.0)),
    ).astype(BF16)
    for q in range(group_count):
        b = b_ref[0, :, q * N:(q + 1) * N]
        c = c_ref[0, :, q * N:(q + 1) * N]
        contract = (((1,), (1,)), ((), ()))
        cross_up = lax.dot_general(c, b, contract, preferred_element_type=F32)
        cross_down = lax.dot_general(b, c, contract, preferred_element_type=F32)
        high, low = split(jnp.where(link_up, cross_up, 0.0))
        lhs_up[q, 0:length, 0:length] = high
        lhs_up[q, 0:length, length:] = high
        low_up[q] = low
        high, low = split(jnp.where(link_down, cross_down, 0.0))
        lhs_down[q, 0:length, 0:length] = high
        lhs_down[q, 0:length, length:] = high
        low_down[q] = low
        b_kept = b.astype(F32) * out_mask
        c_kept = c.astype(F32) * in_mask
        b_turned = b_kept.T.astype(BF16)
        c_turned = c_kept.T.astype(BF16)
        lhs_up[q, length:, 0:length] = b_turned
        lhs_up[q, length:, length:] = b_turned
        lhs_down[q, length:, 0:length] = c_turned
        lhs_down[q, length:, length:] = c_turned
        enter_up[q, :, 0:N] = c_kept.astype(BF16)
        enter_up[q, :, N:] = c_kept.astype(BF16)
        enter_down[q, :, 0:N] = b_kept.astype(BF16)
        enter_down[q, :, N:] = b_kept.astype(BF16)

    def factors(j):
        own = lax.broadcasted_iota(jnp.int32, (heads, cols), 0)
        lane = lax.broadcasted_iota(jnp.int32, (heads, cols), 1)
        first = own * P_SIZE - j * cols
        pick = jnp.logical_and(lane >= first, lane < first + P_SIZE)
        wide = dot(small[...], jnp.where(pick, 1.0, 0.0).astype(BF16))
        decay = wide[0:length]
        gain_wide = jnp.sum(wide[length:], axis=0, keepdims=True)
        shift = dot(centre[...], decay.astype(BF16))
        half = decay[0:1] - shift[0:1]
        return shift, half, gain_wide

    steps = chunks + LAG * (seq_count - 1) + UP_DELAY

    @pl.loop(0, steps)
    def _(step):
        ju = step - UP_DELAY - LAG * seq
        jd = step - LAG * (seq_count - 1 - seq)
        up_on = jnp.logical_and(ju >= 0, ju < chunks)
        down_on = jnp.logical_and(jd >= 0, jd < chunks)

        def relay(on, j, source, target, copies, code_in, scale_in, code_out, scale_out, got, own):
            @pl.when(on)
            def _():
                @pl.when(jnp.logical_not(source))
                def _():
                    got[...] = jnp.zeros(got.shape, F32)

                @pl.when(source)
                def _():
                    for copy in copies(j):
                        copy.wait_recv()
                    scale = jnp.sum(
                        jnp.where(row == col, scale_in[j, 0:1], 0.0), axis=1, keepdims=True
                    )
                    got[...] = code_in[j].astype(jnp.int32).astype(F32) * scale

                @pl.when(target)
                def _():
                    state = got[...] * own[j, N:N + 1] + own[j, 0:N]
                    largest = jnp.maximum(
                        jnp.max(jnp.abs(state), axis=1, keepdims=True), 1e-30
                    )
                    code = jnp.round(state * (CODE_MAX / largest))
                    code_out[j] = code.astype(jnp.int32).astype(jnp.int16)
                    scale = jnp.sum(
                        jnp.where(row == col, largest * (1.0 / CODE_MAX), 0.0),
                        axis=0, keepdims=True,
                    )
                    scale_out[j] = jnp.broadcast_to(scale, scale_out.shape[1:])
                    for copy in copies(j):
                        copy.start()

        @pl.when(step < chunks)
        def _():
            j = step
            q = j // chunks_per_group
            shift, half, gain_wide = factors(j)
            forth, back = jnp.exp(shift), jnp.exp(-shift)
            forth_end, forth_in = jnp.exp(shift[length - 1:]), jnp.exp(half)
            gone = jnp.exp(half + shift[length - 1:]) * gone_row[0:1, 0:1]
            g = g_ref[0, :, pl.ds(pl.multiple_of(j * cols, cols), cols)].astype(F32)
            high, low = split(g * forth)
            both = dot(lhs_down[q], jnp.concatenate([high, low], axis=0))
            part_down[j, 0] = (both[0:length] + dot(low_down[q], high)) * back + gain_wide * g
            part_down[j, 1] = back * forth_end
            own_down[j, 0:N] = both[length:] * forth_in
            own_down[j, N:N + 8] = jnp.broadcast_to(gone, (8, cols))

        relay(down_on, jd, has_next, has_prev, down_copies, down_in, down_scale_in,
              down_out, down_scale_out, got_down, own_down)

        j_up = step - UP_DELAY

        @pl.when(jnp.logical_and(j_up >= 0, j_up < chunks))
        def _():
            j = j_up
            q = j // chunks_per_group
            shift, half, gain_wide = factors(j)
            forth, back = jnp.exp(shift), jnp.exp(-shift)
            forth_end, forth_in = jnp.exp(shift[length - 1:]), jnp.exp(half)
            gone = jnp.exp(half + shift[length - 1:]) * gone_row[0:1, 0:1]

            @pl.when(pipe == 0)
            def _():
                x_buf[j] = e_ref[0, :, pl.ds(pl.multiple_of(j * cols, cols), cols)]

            @pl.when(has_prev_pipe)
            def _():
                x_copy(j).wait_recv()

            x = x_buf[j].astype(F32)
            high, low = split(x * back)
            both = dot(lhs_up[q], jnp.concatenate([high, low], axis=0))
            part_up[j, 0] = (both[0:length] + dot(low_up[q], high)) * forth + gain_wide * x
            part_up[j, 1] = forth * forth_in
            own_up[j, 0:N] = both[length:] * forth_end
            own_up[j, N:N + 8] = jnp.broadcast_to(gone, (8, cols))

        relay(up_on, ju, has_prev, has_next, up_copies, up_in, up_scale_in,
              up_out, up_scale_out, got_up, own_up)

        @pl.when(down_on)
        def _():
            q = jd // chunks_per_group
            both = jnp.concatenate(split(got_down[...]), axis=0)
            total = part_down[jd, 0] + dot(enter_down[q], both) * part_down[jd, 1]
            grad_ref[0, :, pl.ds(pl.multiple_of(jd * cols, cols), cols)] = total.astype(BF16)

        @pl.when(up_on)
        def _():
            q = ju // chunks_per_group
            both = jnp.concatenate(split(got_up[...]), axis=0)
            total = part_up[ju, 0] + dot(enter_up[q], both) * part_up[ju, 1]
            mixed_ref[0, :, pl.ds(pl.multiple_of(ju * cols, cols), cols)] = total.astype(BF16)

    @pl.loop(0, chunks)
    def _(j):
        @pl.when(has_next_pipe)
        def _():
            x_copy(j).wait_send()

        @pl.when(has_next)
        def _():
            for copy in up_copies(j):
                copy.wait_send()

        @pl.when(has_prev)
        def _():
            for copy in down_copies(j):
                copy.wait_send()


def body(pipe_count, seq_count, emitted, cotangent, b_proj, c_proj, log_decay, starts, skip):
    _, length, width = emitted.shape
    heads = skip.shape[1]
    group_count = b_proj.shape[2] // N
    cols = COLS
    chunks = width // cols
    whole = pl.BlockSpec(memory_space=pltpu.VMEM)
    dma = pltpu.SemaphoreType.DMA
    return pl.pallas_call(
        functools.partial(kernel, pipe_count, seq_count, cols),
        out_shape=(
            jax.ShapeDtypeStruct(emitted.shape, BF16),
            jax.ShapeDtypeStruct(emitted.shape, BF16),
        ),
        in_specs=[whole] * 7,
        out_specs=(whole, whole),
        scratch_shapes=[
            pltpu.VMEM((chunks, length, cols), BF16),
            pltpu.VMEM((chunks, N, cols), jnp.int16),
            pltpu.VMEM((chunks, N, cols), jnp.int16),
            pltpu.VMEM((chunks, N, cols), jnp.int16),
            pltpu.VMEM((chunks, N, cols), jnp.int16),
            pltpu.VMEM((chunks, 8, N), F32),
            pltpu.VMEM((chunks, 8, N), F32),
            pltpu.VMEM((chunks, 8, N), F32),
            pltpu.VMEM((chunks, 8, N), F32),
            pltpu.VMEM((N, cols), F32),
            pltpu.VMEM((N, cols), F32),
            pltpu.VMEM((length + 16, heads), BF16),
            pltpu.VMEM((length, length), BF16),
            pltpu.VMEM((group_count, length + N, 2 * length), BF16),
            pltpu.VMEM((group_count, length + N, 2 * length), BF16),
            pltpu.VMEM((group_count, length, length), BF16),
            pltpu.VMEM((group_count, length, length), BF16),
            pltpu.VMEM((group_count, length, 2 * N), BF16),
            pltpu.VMEM((group_count, length, 2 * N), BF16),
            pltpu.VMEM((chunks, 2, length, cols), F32),
            pltpu.VMEM((chunks, 2, length, cols), F32),
            pltpu.VMEM((chunks, N + 8, cols), F32),
            pltpu.VMEM((chunks, N + 8, cols), F32),
            pltpu.VMEM((8, 128), F32),
            dma((chunks,)), dma((chunks,)), dma((chunks,)),
            dma((chunks,)), dma((chunks,)), dma((chunks,)),
            dma((chunks,)), dma((chunks,)), dma((chunks,)), dma((chunks,)),
        ],
        compiler_params=pltpu.CompilerParams(
            collective_id=0, has_side_effects=True, vmem_limit_bytes=40 * 1024 * 1024
        ),
    )(emitted, cotangent, b_proj, c_proj, log_decay, starts, skip)


def solution(mesh):
    wide = P("pipe", "seq", "tp")
    return jax.shard_map(
        functools.partial(body, mesh.shape["pipe"], mesh.shape["seq"]),
        mesh=mesh,
        in_specs=(wide, wide, wide, wide, wide, P("pipe", "seq"), P("pipe", "tp")),
        out_specs=(wide, wide),
        check_vma=False,
    )
```

```python
import functools

import jax
import jax.numpy as jnp
from jax import lax
from jax.experimental import pallas as pl
from jax.experimental.pallas import tpu as pltpu
from jax.sharding import PartitionSpec as P

BLEND_CHANNELS = 128
P_SIZE = 64
CODE_MAX = 32000.0
N = 128
GROUPS = 4
COLS = 512
LAG = 2
UP_DELAY = 0
MESH = pl.DeviceIdType.MESH
F32 = jnp.float32
BF16 = jnp.bfloat16


def split(value):
    high = value.astype(BF16)
    return high, (value - high.astype(F32)).astype(BF16)


def dot(a, b):
    return jnp.dot(a, b, preferred_element_type=F32)


def kernel(
    pipe_count, seq_count, cols,
    e_ref, g_ref, b_ref, c_ref, d_ref, st_ref, sk_ref,
    mixed_ref, grad_ref,
    x_buf, up_out, up_in, down_out, down_in,
    up_scale_out, up_scale_in, down_scale_out, down_scale_in, got_up, got_down,
    small, centre, lhs_up, lhs_down, low_up, low_down, enter_up, enter_down,
    part_up, part_down, own_up, own_down, gone_row,
    x_send, x_recv, up_send, up_recv, down_send, down_recv,
    up_scale_send, up_scale_recv, down_scale_send, down_scale_recv,
):
    length = e_ref.shape[1]
    chunks = e_ref.shape[2] // cols
    heads = sk_ref.shape[1]
    group_count = b_ref.shape[2] // N
    chunk_heads = cols // P_SIZE
    chunks_per_group = chunks // group_count
    middle = length // 2 - 1
    pipe = lax.axis_index("pipe")
    seq = lax.axis_index("seq")
    has_prev_pipe, has_next_pipe = pipe > 0, pipe < pipe_count - 1
    has_prev, has_next = seq > 0, seq < seq_count - 1

    barrier = pltpu.get_barrier_semaphore()

    def greet(present, where):
        @pl.when(present)
        def _():
            pl.semaphore_signal(barrier, inc=1, device_id=where, device_id_type=MESH)

    greet(has_prev_pipe, {"pipe": pipe - 1})
    greet(has_next_pipe, {"pipe": pipe + 1})
    greet(has_prev, {"seq": seq - 1})
    greet(has_next, {"seq": seq + 1})
    count = (
        has_prev_pipe.astype(jnp.int32) + has_next_pipe.astype(jnp.int32)
        + has_prev.astype(jnp.int32) + has_next.astype(jnp.int32)
    )
    pl.semaphore_wait(barrier, count)

    def x_copy(j):
        return pltpu.make_async_remote_copy(
            src_ref=e_ref.at[0, :, pl.ds(pl.multiple_of(j * cols, cols), cols)],
            dst_ref=x_buf.at[j],
            send_sem=x_send.at[j], recv_sem=x_recv.at[j],
            device_id={"pipe": pipe + 1}, device_id_type=MESH,
        )

    def pair(pieces, where):
        return [
            pltpu.make_async_remote_copy(
                src_ref=source, dst_ref=target, send_sem=sent, recv_sem=arrived,
                device_id=where, device_id_type=MESH,
            )
            for source, target, sent, arrived in pieces
        ]

    def up_copies(j):
        return pair([
            (up_scale_out.at[j], up_scale_in.at[j], up_scale_send.at[j], up_scale_recv.at[j]),
            (up_out.at[j], up_in.at[j], up_send.at[j], up_recv.at[j]),
        ], {"seq": seq + 1})

    def down_copies(j):
        return pair([
            (down_scale_out.at[j], down_scale_in.at[j], down_scale_send.at[j],
             down_scale_recv.at[j]),
            (down_out.at[j], down_in.at[j], down_send.at[j], down_recv.at[j]),
        ], {"seq": seq - 1})

    @pl.when(has_next_pipe)
    def _():
        @pl.loop(0, chunks)
        def _(j):
            x_copy(j).start()

    row = lax.broadcasted_iota(jnp.int32, (length, length), 0)
    col = lax.broadcasted_iota(jnp.int32, (length, length), 1)
    starts_row = st_ref[...].astype(F32)
    starts_col = jnp.sum(jnp.where(row == col, starts_row, 0.0), axis=1, keepdims=True)
    opened_col = jnp.sum(jnp.where(col <= row, starts_row, 0.0), axis=1, keepdims=True)
    opened_row = jnp.sum(jnp.where(row <= col, starts_col, 0.0), axis=0, keepdims=True)
    opened_end = jnp.sum(starts_row, axis=1, keepdims=True)
    same = opened_col == opened_row
    link_up = jnp.logical_and(same, col <= row)
    link_down = jnp.logical_and(same, row <= col)
    in_mask = jnp.where(opened_col == 0.0, 1.0, 0.0)
    out_mask = jnp.where(opened_col == opened_end, 1.0, 0.0)
    gone_row[...] = jnp.broadcast_to(jnp.where(opened_end == 0.0, 1.0, 0.0), gone_row.shape)
    centre[...] = (
        jnp.where(col <= row, 1.0, 0.0) - jnp.where(col <= middle, 1.0, 0.0)
    ).astype(BF16)
    small[0:length, :] = d_ref[0]
    gain = sk_ref[...]
    gain_high = gain.astype(BF16).astype(F32)
    gain_mid = (gain - gain_high).astype(BF16).astype(F32)
    gain_low = gain - gain_high - gain_mid
    gain_row = lax.broadcasted_iota(jnp.int32, (16, heads), 0)
    small[length:, :] = jnp.where(
        gain_row == 0, gain_high,
        jnp.where(gain_row == 1, gain_mid, jnp.where(gain_row == 2, gain_low, 0.0)),
    ).astype(BF16)
    for q in range(group_count):
        b = b_ref[0, :, q * N:(q + 1) * N]
        c = c_ref[0, :, q * N:(q + 1) * N]
        contract = (((1,), (1,)), ((), ()))
        cross_up = lax.dot_general(c, b, contract, preferred_element_type=F32)
        cross_down = lax.dot_general(b, c, contract, preferred_element_type=F32)
        high, low = split(jnp.where(link_up, cross_up, 0.0))
        lhs_up[q, 0:length, 0:length] = high
        lhs_up[q, 0:length, length:] = high
        low_up[q] = low
        high, low = split(jnp.where(link_down, cross_down, 0.0))
        lhs_down[q, 0:length, 0:length] = high
        lhs_down[q, 0:length, length:] = high
        low_down[q] = low
        b_kept = b.astype(F32) * out_mask
        c_kept = c.astype(F32) * in_mask
        b_turned = b_kept.T.astype(BF16)
        c_turned = c_kept.T.astype(BF16)
        lhs_up[q, length:, 0:length] = b_turned
        lhs_up[q, length:, length:] = b_turned
        lhs_down[q, length:, 0:length] = c_turned
        lhs_down[q, length:, length:] = c_turned
        enter_up[q, :, 0:N] = c_kept.astype(BF16)
        enter_up[q, :, N:] = c_kept.astype(BF16)
        enter_down[q, :, 0:N] = b_kept.astype(BF16)
        enter_down[q, :, N:] = b_kept.astype(BF16)

    def factors(j):
        own = lax.broadcasted_iota(jnp.int32, (heads, cols), 0)
        lane = lax.broadcasted_iota(jnp.int32, (heads, cols), 1)
        first = own * P_SIZE - j * cols
        pick = jnp.logical_and(lane >= first, lane < first + P_SIZE)
        wide = dot(small[...], jnp.where(pick, 1.0, 0.0).astype(BF16))
        decay = wide[0:length]
        gain_wide = jnp.sum(wide[length:], axis=0, keepdims=True)
        shift = dot(centre[...], decay.astype(BF16))
        half = decay[0:1] - shift[0:1]
        return shift, half, gain_wide

    steps = chunks + LAG * (seq_count - 1) + UP_DELAY

    @pl.loop(0, steps)
    def _(step):
        ju = step - UP_DELAY - LAG * seq
        jd = step - LAG * (seq_count - 1 - seq)
        up_on = jnp.logical_and(ju >= 0, ju < chunks)
        down_on = jnp.logical_and(jd >= 0, jd < chunks)

        def relay(on, j, source, target, copies, code_in, scale_in, code_out, scale_out, got, own):
            @pl.when(on)
            def _():
                @pl.when(jnp.logical_not(source))
                def _():
                    got[...] = jnp.zeros(got.shape, F32)

                @pl.when(source)
                def _():
                    for copy in copies(j):
                        copy.wait_recv()
                    scale = jnp.sum(
                        jnp.where(row == col, scale_in[j, 0:1], 0.0), axis=1, keepdims=True
                    )
                    got[...] = code_in[j].astype(jnp.int32).astype(F32) * scale

                @pl.when(target)
                def _():
                    state = got[...] * own[j, N:N + 1] + own[j, 0:N]
                    largest = jnp.maximum(
                        jnp.max(jnp.abs(state), axis=1, keepdims=True), 1e-30
                    )
                    code = jnp.round(state * (CODE_MAX / largest))
                    code_out[j] = code.astype(jnp.int32).astype(jnp.int16)
                    scale_copy, code_copy = copies(j)
                    code_copy.start()
                    scale = jnp.sum(
                        jnp.where(row == col, largest * (1.0 / CODE_MAX), 0.0),
                        axis=0, keepdims=True,
                    )
                    scale_out[j] = jnp.broadcast_to(scale, scale_out.shape[1:])
                    scale_copy.start()

        @pl.when(step < chunks)
        def _():
            j = step
            q = j // chunks_per_group
            shift, half, gain_wide = factors(j)
            forth, back = jnp.exp(shift), jnp.exp(-shift)
            forth_end, forth_in = jnp.exp(shift[length - 1:]), jnp.exp(half)
            gone = jnp.exp(half + shift[length - 1:]) * gone_row[0:1, 0:1]
            g = g_ref[0, :, pl.ds(pl.multiple_of(j * cols, cols), cols)].astype(F32)
            high, low = split(g * forth)
            both = dot(lhs_down[q], jnp.concatenate([high, low], axis=0))
            part_down[j, 0] = (both[0:length] + dot(low_down[q], high)) * back + gain_wide * g
            part_down[j, 1] = back * forth_end
            own_down[j, 0:N] = both[length:] * forth_in
            own_down[j, N:N + 8] = jnp.broadcast_to(gone, (8, cols))

        relay(down_on, jd, has_next, has_prev, down_copies, down_in, down_scale_in,
              down_out, down_scale_out, got_down, own_down)

        j_up = step - UP_DELAY

        @pl.when(jnp.logical_and(j_up >= 0, j_up < chunks))
        def _():
            j = j_up
            q = j // chunks_per_group
            shift, half, gain_wide = factors(j)
            forth, back = jnp.exp(shift), jnp.exp(-shift)
            forth_end, forth_in = jnp.exp(shift[length - 1:]), jnp.exp(half)
            gone = jnp.exp(half + shift[length - 1:]) * gone_row[0:1, 0:1]

            @pl.when(pipe == 0)
            def _():
                x_buf[j] = e_ref[0, :, pl.ds(pl.multiple_of(j * cols, cols), cols)]

            @pl.when(has_prev_pipe)
            def _():
                x_copy(j).wait_recv()

            x = x_buf[j].astype(F32)
            high, low = split(x * back)
            both = dot(lhs_up[q], jnp.concatenate([high, low], axis=0))
            part_up[j, 0] = (both[0:length] + dot(low_up[q], high)) * forth + gain_wide * x
            part_up[j, 1] = forth * forth_in
            own_up[j, 0:N] = both[length:] * forth_end
            own_up[j, N:N + 8] = jnp.broadcast_to(gone, (8, cols))

        relay(up_on, ju, has_prev, has_next, up_copies, up_in, up_scale_in,
              up_out, up_scale_out, got_up, own_up)

        @pl.when(down_on)
        def _():
            q = jd // chunks_per_group
            both = jnp.concatenate(split(got_down[...]), axis=0)
            total = part_down[jd, 0] + dot(enter_down[q], both) * part_down[jd, 1]
            grad_ref[0, :, pl.ds(pl.multiple_of(jd * cols, cols), cols)] = total.astype(BF16)

        @pl.when(up_on)
        def _():
            q = ju // chunks_per_group
            both = jnp.concatenate(split(got_up[...]), axis=0)
            total = part_up[ju, 0] + dot(enter_up[q], both) * part_up[ju, 1]
            mixed_ref[0, :, pl.ds(pl.multiple_of(ju * cols, cols), cols)] = total.astype(BF16)

    @pl.loop(0, chunks)
    def _(j):
        @pl.when(has_next_pipe)
        def _():
            x_copy(j).wait_send()

        @pl.when(has_next)
        def _():
            for copy in up_copies(j):
                copy.wait_send()

        @pl.when(has_prev)
        def _():
            for copy in down_copies(j):
                copy.wait_send()


def body(pipe_count, seq_count, emitted, cotangent, b_proj, c_proj, log_decay, starts, skip):
    _, length, width = emitted.shape
    heads = skip.shape[1]
    group_count = b_proj.shape[2] // N
    cols = COLS
    chunks = width // cols
    whole = pl.BlockSpec(memory_space=pltpu.VMEM)
    dma = pltpu.SemaphoreType.DMA
    return pl.pallas_call(
        functools.partial(kernel, pipe_count, seq_count, cols),
        out_shape=(
            jax.ShapeDtypeStruct(emitted.shape, BF16),
            jax.ShapeDtypeStruct(emitted.shape, BF16),
        ),
        in_specs=[whole] * 7,
        out_specs=(whole, whole),
        scratch_shapes=[
            pltpu.VMEM((chunks, length, cols), BF16),
            pltpu.VMEM((chunks, N, cols), jnp.int16),
            pltpu.VMEM((chunks, N, cols), jnp.int16),
            pltpu.VMEM((chunks, N, cols), jnp.int16),
            pltpu.VMEM((chunks, N, cols), jnp.int16),
            pltpu.VMEM((chunks, 8, N), F32),
            pltpu.VMEM((chunks, 8, N), F32),
            pltpu.VMEM((chunks, 8, N), F32),
            pltpu.VMEM((chunks, 8, N), F32),
            pltpu.VMEM((N, cols), F32),
            pltpu.VMEM((N, cols), F32),
            pltpu.VMEM((length + 16, heads), BF16),
            pltpu.VMEM((length, length), BF16),
            pltpu.VMEM((group_count, length + N, 2 * length), BF16),
            pltpu.VMEM((group_count, length + N, 2 * length), BF16),
            pltpu.VMEM((group_count, length, length), BF16),
            pltpu.VMEM((group_count, length, length), BF16),
            pltpu.VMEM((group_count, length, 2 * N), BF16),
            pltpu.VMEM((group_count, length, 2 * N), BF16),
            pltpu.VMEM((chunks, 2, length, cols), F32),
            pltpu.VMEM((chunks, 2, length, cols), F32),
            pltpu.VMEM((chunks, N + 8, cols), F32),
            pltpu.VMEM((chunks, N + 8, cols), F32),
            pltpu.VMEM((8, 128), F32),
            dma((chunks,)), dma((chunks,)), dma((chunks,)),
            dma((chunks,)), dma((chunks,)), dma((chunks,)),
            dma((chunks,)), dma((chunks,)), dma((chunks,)), dma((chunks,)),
        ],
        compiler_params=pltpu.CompilerParams(
            collective_id=0, has_side_effects=True, vmem_limit_bytes=40 * 1024 * 1024
        ),
    )(emitted, cotangent, b_proj, c_proj, log_decay, starts, skip)


def solution(mesh):
    wide = P("pipe", "seq", "tp")
    return jax.shard_map(
        functools.partial(body, mesh.shape["pipe"], mesh.shape["seq"]),
        mesh=mesh,
        in_specs=(wide, wide, wide, wide, wide, P("pipe", "seq"), P("pipe", "tp")),
        out_specs=(wide, wide),
        check_vma=False,
    )
```
